128 devices in a mesh: aux: 16 (over y, x), row: 4 (over z), col: 2 (over core).
Axes of the slice: x: 4, y: 4, z: 4, core: 2. Of those that a mesh axis runs over, the one named last changes fastest.
Arguments:
- integrals: bfloat16 [2560, 64, 4096], P('aux', ('row', 'col')), may hold values from -6 to 6
- pair_blocks: int32 [2, 64], P(None, ('row', 'col')), may hold values from -1 to 15, as said below
- occupied: bfloat16 [1024, 64], P('col'), may hold values from -0.75 to 0.75
- metric: bfloat16 [2560, 2560], replicated, as said below
Outputs:
- exchange_k: float32 [1024, 1024], P('row', ('aux', 'col'))
The draws below stay inside these ranges and needn't reach their ends.
Inputs may be any that keep to these rules, and one draw needn't show every extreme that they name: `pair_blocks`: A slot of row group r and column group c (slots (r * number of column groups + c) * 8 onward) is empty (-1 in both entries) or names a row block of r's 4 blocks and a column block of c's 8 blocks; no block pair is named twice; live slots of a group come before its empty ones; every group has 4 or more live slots and some group has all 8 live. `metric`: symmetric.
All inputs are finite; a program needn't handle non-finite values.
Results may differ from the reference program's by a relative error of at most 0.0003.
Values sent between devices are 32-bit elements; how exact they have to be, the bound alone decides.
No kernel may reach another device: no remote copies, remote signals or barrier semaphores. Data moves between devices by JAX's collectives and lax.ppermute only.
A program may use at most 128 MiB of HBM per device.

```python
import jax
import jax.numpy as jnp
from jax import lax

NAUX = 2560
NBF = 1024
NOCC = 64
BS = 64
CAP = 8
NRB = 4
NCB = 8
SLOTS = 64
N_ROW = 4
N_COL = 2


def draw_pair_blocks(key, part):
    groups = N_ROW * N_COL
    per_group = NRB * NCB
    key_count, key_forced, key_score = jax.random.split(jax.random.fold_in(key, 11), 3)
    counts = jax.random.randint(key_count, (groups,), max(1, CAP // 2), CAP + 1)
    forced = jax.random.randint(key_forced, (), 0, groups)
    counts = jnp.where(jnp.arange(groups) == forced, CAP, counts)
    scores = jax.random.randint(key_score, (groups, per_group), 0, 1 << 20) * per_group + jnp.arange(per_group)[None, :]
    ranked = jnp.argsort(scores, axis=1)[:, :CAP]
    group_row = jnp.arange(groups) // N_COL
    group_col = jnp.arange(groups) % N_COL
    row_ids = group_row[:, None] * NRB + ranked // NCB
    col_ids = group_col[:, None] * NCB + ranked % NCB
    filled = jnp.arange(CAP)[None, :] < counts[:, None]
    row_ids = jnp.where(filled, row_ids, -1)
    col_ids = jnp.where(filled, col_ids, -1)
    return jnp.stack([row_ids.reshape(-1), col_ids.reshape(-1)]).astype(jnp.int32)


def draw_metric(key, part):
    key_off, key_diag = jax.random.split(jax.random.fold_in(key, 23))
    factor = (NAUX * NOCC) ** (-0.25)
    raw = jax.random.normal(key_off, (NAUX, NAUX), jnp.float32)
    diag = jnp.exp(jax.random.uniform(key_diag, (NAUX,), jnp.float32, -0.7, 0.7))
    sym = (raw + raw.T) * (0.35 / jnp.sqrt(jnp.float32(NAUX)))
    matrix = sym * (1.0 - jnp.eye(NAUX, dtype=jnp.float32)) + jnp.diag(diag)
    return (matrix * factor).astype(jnp.bfloat16)


def steps_of(own_key, extent, cuts, low, top_value):
    loudness, own = 1.0, jax.random.fold_in(own_key, 6)
    for dim, blocks in cuts:
        draws = jnp.exp(jax.random.uniform(jax.random.fold_in(own, dim), (blocks,), jnp.float32, low / len(cuts), top_value / len(cuts)))
        loudness = loudness * jnp.repeat(draws, extent[dim] // blocks).reshape([-1 if axis == dim else 1 for axis in range(len(extent))])
    return loudness


def centred(key, shape, deviation, limit, cuts=(), kind=jnp.bfloat16):
    level = steps_of(key, shape, cuts, -0.22, 0.18) if cuts else 1.0
    entries = jax.random.normal(key, shape, jnp.float32) * deviation * level
    return jnp.minimum(jnp.maximum(entries, -limit), limit).astype(kind)


def setup_inputs(seed: int = 0) -> dict:
    streams_of = jax.random.split(jax.random.key(seed), 5)
    integrals = centred(streams_of[0], (NAUX, SLOTS, BS * BS), 1.0, 6.0, ((0, 16), (1, 8)))
    pair_blocks = draw_pair_blocks(jax.random.fold_in(streams_of[4], 71), 0)
    occupied = centred(streams_of[2], (NBF, NOCC), 0.125, 0.75, ((0, 2),))
    metric = draw_metric(jax.random.fold_in(streams_of[4], 71), 0)
    return dict(integrals=integrals, pair_blocks=pair_blocks, occupied=occupied, metric=metric)


def reference(integrals, pair_blocks, occupied, metric):
    width = min(8, NOCC)
    count = NOCC // width
    zero_index = jnp.zeros((), jnp.int32)
    metric_wide = metric.astype(jnp.float32)

    def one_block(total, index):
        coeffs = lax.dynamic_slice_in_dim(occupied, (index * width).astype(jnp.int32), width, 1).astype(jnp.float32)

        def add_slot(carry, slot):
            row_block = pair_blocks[0, slot]
            col_block = pair_blocks[1, slot]
            filled = (row_block >= 0).astype(jnp.float32)
            safe_row = jnp.maximum(row_block, 0).astype(jnp.int32)
            safe_col = jnp.maximum(col_block, 0).astype(jnp.int32)
            tile = lax.dynamic_index_in_dim(integrals, slot, 1, False).astype(jnp.float32).reshape(NAUX, BS, BS)
            cpart = lax.dynamic_slice_in_dim(coeffs, (safe_col * BS).astype(jnp.int32), BS, 0)
            piece = jnp.einsum('pmn,ni->pmi', tile, cpart, precision=lax.Precision.HIGHEST) * filled
            starts = (zero_index, (safe_row * BS).astype(jnp.int32), zero_index)
            current = lax.dynamic_slice(carry, starts, (NAUX, BS, width))
            carry = lax.dynamic_update_slice(carry, current + piece, starts)
            return carry, None

        start = jnp.zeros((NAUX, NBF, width), jnp.float32)
        half, _ = lax.scan(add_slot, start, jnp.arange(SLOTS, dtype=jnp.int32))
        fitted = jnp.dot(metric_wide, half.reshape(NAUX, NBF * width), precision=lax.Precision.HIGHEST, preferred_element_type=jnp.float32)
        fitted = fitted.reshape(NAUX, NBF, width)
        flat = jnp.transpose(fitted, (1, 0, 2)).reshape(NBF, NAUX * width)
        total = total + jnp.dot(flat, flat.T, precision=lax.Precision.HIGHEST, preferred_element_type=jnp.float32)
        return total, None

    result, _ = lax.scan(one_block, jnp.zeros((NBF, NBF), jnp.float32), jnp.arange(count, dtype=jnp.int32))
    return result
```

```python
import functools

import jax
import jax.numpy as jnp
from jax import lax
from jax.experimental import pallas as pl
from jax.experimental.pallas import tpu as pltpu
from jax.sharding import PartitionSpec as P

BS = 64
SLOT = 8
NOCC = 64
NAUX = 2560
AUX = 160
GROUPS = 16
CHUNKS = ((0, 80), (80, 80))
PB = 16
TILE = 512
F32 = jnp.float32
BF16 = jnp.bfloat16


def half_kernel(pairs, x_ref, occ_ref, mine_ref, other_ref, weights, wide, rhs, prod):
    @pl.when(pl.program_id(0) == 0)
    def _():
        core = lax.axis_index("col")
        row = lax.broadcasted_iota(jnp.int32, (8 * BS, 2 * BS), 0)
        lane = lax.broadcasted_iota(jnp.int32, (8 * BS, 2 * BS), 1)
        own = lax.broadcasted_iota(jnp.int32, (BS, 2 * BS), 1)
        for s in range(SLOT):
            b, e = pairs[0, s], pairs[1, s]
            local_b = jnp.where(b >= 0, lax.rem(b + 64, 4), 0)
            local_e = lax.rem(e + 64, 8)
            place = lax.rem(local_b // 2 + core, 2) * 2 + lax.rem(local_b, 2)
            place = jnp.where(b >= 0, place, -1)
            pick = jnp.where(row == local_e * BS + lax.rem(lane, BS), 1.0, 0.0).astype(BF16)
            c = jnp.dot(occ_ref[...], pick, preferred_element_type=F32)
            for hb in range(4):
                keep = jnp.where(place == hb, 1.0, 0.0)
                for m2 in range(2):
                    part = jnp.where(own // BS == m2, c, 0.0) * keep
                    at = (hb * 2 + m2) * BS
                    weights[at : at + BS, s * 128 : (s + 1) * 128] = part.astype(BF16)

    for j in range(32):
        wide[:, j] = x_ref[:, :, j * 128 : (j + 1) * 128].astype(F32)
    flat = wide.reshape(PB * 32 * SLOT, 128)
    for s in range(SLOT):
        rhs[:, s * 128 : (s + 1) * 128] = flat[pl.ds(s, PB * 32, stride=SLOT), :].astype(BF16)
    prod[...] = lax.dot_general(
        weights[...], rhs[...], (((1,), (1,)), ((), ())), preferred_element_type=F32
    )
    lane = lax.broadcasted_iota(jnp.int32, (NOCC, 128), 1)
    low64 = lane < 64
    low32 = lax.rem(lane, 64) < 32
    for h, ref in ((0, mine_ref), (1, other_ref)):
        out = ref.reshape(NOCC * PB, 128)
        for q in range(PB // 4):
            t = [prod[(h * 4 + k) * BS : (h * 4 + k + 1) * BS, q * 128 : (q + 1) * 128] for k in range(4)]
            r = [pltpu.roll(v, 64, 1) for v in t]
            a0 = jnp.where(low64, t[0], r[2])
            a2 = jnp.where(low64, r[0], t[2])
            a1 = jnp.where(low64, t[1], r[3])
            a3 = jnp.where(low64, r[1], t[3])
            for p, (u, v) in enumerate(((a0, a1), (a2, a3))):
                out[pl.ds(q * 4 + p * 2, NOCC, stride=PB), :] = jnp.where(low32, u, pltpu.roll(v, 32, 1))
                out[pl.ds(q * 4 + p * 2 + 1, NOCC, stride=PB), :] = jnp.where(low32, pltpu.roll(u, 96, 1), v)


def half_transform(integrals, pair_blocks, occ, start, size):
    first = start // PB
    out = jax.ShapeDtypeStruct((NOCC, size, 128), F32)
    block = pl.BlockSpec((NOCC, PB, 128), lambda g, pairs: (0, g, 0))
    return pl.pallas_call(
        half_kernel,
        out_shape=(out, out),
        grid_spec=pltpu.PrefetchScalarGridSpec(
            num_scalar_prefetch=1,
            grid=(size // PB,),
            in_specs=[
                pl.BlockSpec((PB, SLOT, BS * BS), lambda g, pairs: (g + first, 0, 0)),
                pl.BlockSpec((NOCC, 8 * BS), lambda g, pairs: (0, 0)),
            ],
            out_specs=(block, block),
            scratch_shapes=[
                pltpu.VMEM((8 * BS, SLOT * 128), BF16),
                pltpu.VMEM((PB, 32, SLOT, 128), F32),
                pltpu.VMEM((PB * 32, SLOT * 128), BF16),
                pltpu.VMEM((8 * BS, PB * 32), F32),
            ],
        ),
        compiler_params=pltpu.CompilerParams(vmem_limit_bytes=56 << 20),
        cost_estimate=pl.CostEstimate(flops=2 * size * 32 * 1024 * 512, bytes_accessed=size * 131072, transcendentals=0),
        name="half_transform",
    )(pair_blocks, integrals, occ)


def load(src, dst, sem, parts):
    step = src.shape[0] // parts
    return [
        pltpu.make_async_copy(src.at[pl.ds(k * step, step)], dst.at[pl.ds(k * step, step)], sem.at[k])
        for k in range(parts)
    ]


def tiles(metric_ref, rows, sem, start, size):
    return [
        pltpu.make_async_copy(
            metric_ref.at[:, pl.ds(start, size), pl.ds(n * TILE, TILE)], rows.at[:, :, pl.ds(n * TILE, TILE)], sem.at[n]
        )
        for n in range(NAUX // TILE)
    ]


def turn(buf, high, low):
    for r in range(4):
        t = jnp.concatenate([buf[a * 4 + r] for a in range(GROUPS)], axis=0).T
        top = t.astype(BF16)
        high[r * 128 : (r + 1) * 128, :] = top
        if low is not None:
            low[r * 128 : (r + 1) * 128, :] = (t - top.astype(F32)).astype(BF16)


def fit_kernel(start, size, own_ref, oth_ref, metric_ref, fit_ref, rows, buf, high, low, sem, hsem):
    depth = GROUPS * size
    metric = tiles(metric_ref, rows, sem, start, size)
    sides = [load(ref, buf.at[k], hsem.at[k], 4) for k, ref in enumerate((own_ref, oth_ref))]
    for c in (*sides[0], *sides[1], *metric):
        c.start()
    for k in range(2):
        for c in sides[k]:
            c.wait()
        turn(buf.at[k], high.at[k], low.at[k])
    for n in range(NAUX // TILE):
        metric[n].wait()
        m = rows[:, :, n * TILE : (n + 1) * TILE].reshape(depth, TILE)
        for k in range(2):
            fit_ref[k, :, n * TILE : (n + 1) * TILE] = jnp.dot(
                high[k], m, preferred_element_type=F32
            ) + jnp.dot(low[k], m, preferred_element_type=F32)


def first_fit(own, oth, metric, start, size):
    depth = GROUPS * size
    hbm = pl.BlockSpec(memory_space=pl.ANY)
    return pl.pallas_call(
        functools.partial(fit_kernel, start, size),
        out_shape=jax.ShapeDtypeStruct((2, 512, NAUX), F32),
        in_specs=[hbm, hbm, hbm],
        out_specs=pl.BlockSpec(memory_space=pltpu.VMEM),
        scratch_shapes=[
            pltpu.VMEM((GROUPS, size, NAUX), BF16),
            pltpu.VMEM((2, 64, size, 128), F32),
            pltpu.VMEM((2, 512, depth), BF16),
            pltpu.VMEM((2, 512, depth), BF16),
            pltpu.SemaphoreType.DMA((NAUX // TILE,)),
            pltpu.SemaphoreType.DMA((2, 4)),
        ],
        compiler_params=pltpu.CompilerParams(vmem_limit_bytes=46 << 20),
        cost_estimate=pl.CostEstimate(flops=4 * depth * NAUX * 1024, bytes_accessed=24 << 20, transcendentals=0),
        name="first_fit",
    )(own, oth, metric)


def own_kernel(start, size, h_ref, part_ref, metric_ref, fit_ref, rows, buf, part, high, sem, hsem, psem):
    depth = GROUPS * size
    metric = tiles(metric_ref, rows, sem, start, size)
    side = load(h_ref, buf, hsem, 4)
    add = pltpu.make_async_copy(part_ref.at[0], part, psem)
    for c in (*side, *metric, add):
        c.start()
    for c in side:
        c.wait()
    turn(buf, high, None)
    add.wait()
    for n in range(NAUX // TILE):
        metric[n].wait()
        at = slice(n * TILE, (n + 1) * TILE)
        m = rows[:, :, at].reshape(depth, TILE)
        f = part[:, at] + jnp.dot(high[...], m, preferred_element_type=F32)
        top = f.astype(BF16)
        fit_ref[0, :, at] = top
        fit_ref[1, :, at] = (f - top.astype(F32)).astype(BF16)


def own_fit(own, part, metric, start, size):
    depth = GROUPS * size
    hbm = pl.BlockSpec(memory_space=pl.ANY)
    return pl.pallas_call(
        functools.partial(own_kernel, start, size),
        out_shape=jax.ShapeDtypeStruct((2, 512, NAUX), BF16),
        in_specs=[hbm, hbm, hbm],
        out_specs=pl.BlockSpec(memory_space=pltpu.VMEM),
        scratch_shapes=[
            pltpu.VMEM((GROUPS, size, NAUX), BF16),
            pltpu.VMEM((64, size, 128), F32),
            pltpu.VMEM((512, NAUX), F32),
            pltpu.VMEM((512, depth), BF16),
            pltpu.SemaphoreType.DMA((NAUX // TILE,)),
            pltpu.SemaphoreType.DMA((4,)),
            pltpu.SemaphoreType.DMA,
        ],
        compiler_params=pltpu.CompilerParams(vmem_limit_bytes=46 << 20),
        cost_estimate=pl.CostEstimate(flops=2 * depth * NAUX * 512, bytes_accessed=16 << 20, transcendentals=0),
        name="own_fit",
    )(own, part, metric)


def last_kernel(
    start, size, h_ref, part_ref, fit_ref, metric_ref, out_ref, rows, buf, part, own, high, fit, sem, hsem, psem
):
    depth = GROUPS * size
    metric = tiles(metric_ref, rows, sem, start, size)
    side = load(h_ref, buf, hsem, 4)
    add = pltpu.make_async_copy(part_ref.at[1], part, psem.at[0])
    mine = pltpu.make_async_copy(fit_ref, own, psem.at[1])
    for c in (*side, *metric, add, mine):
        c.start()
    for c in side:
        c.wait()
    turn(buf, high, None)
    add.wait()
    for n in range(NAUX // TILE):
        metric[n].wait()
        at = slice(n * TILE, (n + 1) * TILE)
        m = rows[:, :, at].reshape(depth, TILE)
        fit[:, at] = (part[:, at] + jnp.dot(high[...], m, preferred_element_type=F32)).astype(BF16)
    mine.wait()

    core = lax.axis_index("col")
    for other in range(2):
        half = lax.rem(core + other, 2)
        f = fit[...] if other else own[0]
        k = lax.dot_general(f, own[0], (((1,), (1,)), ((), ())), preferred_element_type=F32)
        k = k + lax.dot_general(f, own[1], (((1,), (1,)), ((), ())), preferred_element_type=F32)
        part[:, :512] = k
        for y in range(4):
            for b in range(2):
                for z in range(4):
                    chip = (y * 4 + half * 2 + b) * 4 + z
                    for c in range(2):
                        for m2 in range(2):
                            top = y * 128 + b * 64 + m2 * 32 + c * 16
                            out_ref[chip * 2 + c, m2 * 16 : (m2 + 1) * 16, :] = part[
                                top : top + 16, z * 128 : (z + 1) * 128
                            ]


def last_fit(oth, part, fit, metric, start, size):
    depth = GROUPS * size
    hbm = pl.BlockSpec(memory_space=pl.ANY)
    return pl.pallas_call(
        functools.partial(last_kernel, start, size),
        out_shape=jax.ShapeDtypeStruct((128, 32, 128), F32),
        in_specs=[hbm, hbm, hbm, hbm],
        out_specs=pl.BlockSpec(memory_space=pltpu.VMEM),
        scratch_shapes=[
            pltpu.VMEM((GROUPS, size, NAUX), BF16),
            pltpu.VMEM((64, size, 128), F32),
            pltpu.VMEM((512, NAUX), F32),
            pltpu.VMEM((2, 512, NAUX), BF16),
            pltpu.VMEM((512, depth), BF16),
            pltpu.VMEM((512, NAUX), BF16),
            pltpu.SemaphoreType.DMA((NAUX // TILE,)),
            pltpu.SemaphoreType.DMA((4,)),
            pltpu.SemaphoreType.DMA((2,)),
        ],
        compiler_params=pltpu.CompilerParams(vmem_limit_bytes=46 << 20),
        cost_estimate=pl.CostEstimate(flops=2 * depth * NAUX * 512, bytes_accessed=16 << 20, transcendentals=0),
        name="last_fit",
    )(oth, part, fit, metric)


def sum_kernel(x_ref, out_ref):
    lane_in = lax.broadcasted_iota(jnp.int32, (128, 128), 0)
    lane_out = lax.broadcasted_iota(jnp.int32, (128, 128), 1)
    src = (lane_out // 64) * 64 + lax.rem(lane_out, 2) * 32 + lax.rem(lane_out, 64) // 2
    right = jnp.where(lane_in == src, 1.0, 0.0)
    row_out = lax.broadcasted_iota(jnp.int32, (32, 32), 0)
    row_in = lax.broadcasted_iota(jnp.int32, (32, 32), 1)
    left = jnp.where(row_in == lax.rem(row_out, 2) * 16 + row_out // 2, 1.0, 0.0)
    for h in range(2):
        total = jnp.sum(x_ref[:, h], axis=0)
        total = jnp.dot(total, right, precision=lax.Precision.HIGHEST, preferred_element_type=F32)
        total = jnp.dot(left, total, precision=lax.Precision.HIGHEST, preferred_element_type=F32)
        out_ref[:, h * 128 : (h + 1) * 128] = total


def sum_chips(x):
    return pl.pallas_call(
        sum_kernel,
        out_shape=jax.ShapeDtypeStruct((32, 256), F32),
        compiler_params=pltpu.CompilerParams(vmem_limit_bytes=16 << 20),
        name="sum_chips",
    )(x.reshape(64, 2, 32, 128))


def body(integrals, pair_blocks, occupied, metric):
    occ = occupied.T
    metric = metric.reshape(GROUPS, AUX, NAUX)
    swap = [(0, 1), (1, 0)]
    received = []
    for start, size in CHUNKS:
        mine, other = half_transform(integrals, pair_blocks, occ, start, size)
        h = mine + lax.ppermute(other, "col", swap)
        h, pair_blocks = lax.optimization_barrier((h, pair_blocks))
        received.append(lax.all_to_all(h, ("aux", "row"), 0, 0))
    own, last = received
    part = first_fit(own, lax.ppermute(own, "col", swap), metric, *CHUNKS[0])
    last, part = lax.optimization_barrier((last, part))
    crossed = lax.ppermute(last, "col", swap)
    fit = own_fit(last, part, metric, *CHUNKS[1])
    k = last_fit(crossed, part, fit, metric, *CHUNKS[1])
    k = lax.all_to_all(k, ("aux", "row", "col"), 0, 0)
    return sum_chips(k).T


def solution(mesh):
    return jax.shard_map(
        body,
        mesh=mesh,
        in_specs=(P("aux", ("row", "col"), None), P(None, ("row", "col")), P("col", None), P()),
        out_specs=P("row", ("aux", "col")),
        check_vma=False,
    )
```

```python
import functools

import jax
import jax.numpy as jnp
from jax import lax
from jax.experimental import pallas as pl
from jax.experimental.pallas import tpu as pltpu
from jax.sharding import PartitionSpec as P

BS = 64
SLOT = 8
NOCC = 64
NAUX = 2560
AUX = 160
GROUPS = 16
CHUNKS = ((0, 80), (80, 80))
PB = 16
TILE = 512
F32 = jnp.float32
BF16 = jnp.bfloat16


def half_kernel(start, size, pairs, x_ref, occ_hbm, mine_ref, other_ref, weights, x_buf, wide, rhs, prod, occ_ref, sem, osem):
    copies = [
        pltpu.make_async_copy(x_ref.at[pl.ds(start + g * PB, PB)], x_buf.at[pl.ds(g * PB, PB)], sem.at[g])
        for g in range(size // PB)
    ]
    fetch = pltpu.make_async_copy(occ_hbm, occ_ref, osem)
    fetch.start()
    for c in copies:
        c.start()
    fetch.wait()

    core = lax.axis_index("col")
    row = lax.broadcasted_iota(jnp.int32, (8 * BS, 2 * BS), 0)
    lane = lax.broadcasted_iota(jnp.int32, (8 * BS, 2 * BS), 1)
    own = lax.broadcasted_iota(jnp.int32, (BS, 2 * BS), 1)
    for s in range(SLOT):
        b, e = pairs[0, s], pairs[1, s]
        local_b = jnp.where(b >= 0, lax.rem(b + 64, 4), 0)
        local_e = lax.rem(e + 64, 8)
        place = lax.rem(local_b // 2 + core, 2) * 2 + lax.rem(local_b, 2)
        place = jnp.where(b >= 0, place, -1)
        pick = jnp.where(row == local_e * BS + lax.rem(lane, BS), 1.0, 0.0).astype(BF16)
        c = jnp.dot(occ_ref[...], pick, preferred_element_type=F32)
        for hb in range(4):
            keep = jnp.where(place == hb, 1.0, 0.0)
            for m2 in range(2):
                part = jnp.where(own // BS == m2, c, 0.0) * keep
                at = (hb * 2 + m2) * BS
                weights[at : at + BS, s * 128 : (s + 1) * 128] = part.astype(BF16)

    lane = lax.broadcasted_iota(jnp.int32, (NOCC, 128), 1)
    low64 = lane < 64
    low32 = lax.rem(lane, 64) < 32
    for g in range(size // PB):
        k = g % 2
        copies[g].wait()
        for j in range(32):
            wide[k, :, j] = x_buf[g * PB : (g + 1) * PB, :, j * 128 : (j + 1) * 128].astype(F32)
        flat = wide.at[k].reshape(PB * 32 * SLOT, 128)
        for s in range(SLOT):
            rhs[k, :, s * 128 : (s + 1) * 128] = flat[pl.ds(s, PB * 32, stride=SLOT), :].astype(BF16)
        prod[k] = lax.dot_general(
            weights[...], rhs[k], (((1,), (1,)), ((), ())), preferred_element_type=F32
        )
        for h, ref in ((0, mine_ref), (1, other_ref)):
            out = ref.reshape(NOCC * size, 128)
            for q in range(PB // 4):
                t = [prod[k, (h * 4 + v) * BS : (h * 4 + v + 1) * BS, q * 128 : (q + 1) * 128] for v in range(4)]
                r = [pltpu.roll(jnp.where(low64, t[v + 2], t[v]), 64, 1) for v in range(2)]
                a0, a1 = (jnp.where(low64, t[v], r[v]) for v in range(2))
                a2, a3 = (jnp.where(low64, r[v], t[v + 2]) for v in range(2))
                for p, (u, v) in enumerate(((a0, a1), (a2, a3))):
                    at = g * PB + q * 4 + p * 2
                    out[pl.ds(at, NOCC, stride=size), :] = jnp.where(low32, u, pltpu.roll(v, 32, 1))
                    out[pl.ds(at + 1, NOCC, stride=size), :] = jnp.where(low32, pltpu.roll(u, 96, 1), v)


def half_transform(integrals, pair_blocks, occ, start, size):
    out = jax.ShapeDtypeStruct((NOCC, size, 128), F32)
    vm = pl.BlockSpec(memory_space=pltpu.VMEM)
    hbm = pl.BlockSpec(memory_space=pltpu.HBM)
    return pl.pallas_call(
        functools.partial(half_kernel, start, size),
        out_shape=(out, out),
        in_specs=[pl.BlockSpec(memory_space=pltpu.SMEM), hbm, hbm],
        out_specs=(vm, vm),
        scratch_shapes=[
            pltpu.VMEM((8 * BS, SLOT * 128), BF16),
            pltpu.VMEM((size, SLOT, BS * BS), BF16),
            pltpu.VMEM((2, PB, 32, SLOT, 128), F32),
            pltpu.VMEM((2, PB * 32, SLOT * 128), BF16),
            pltpu.VMEM((2, 8 * BS, PB * 32), F32),
            pltpu.VMEM((NOCC, 8 * BS), BF16),
            pltpu.SemaphoreType.DMA((size // PB,)),
            pltpu.SemaphoreType.DMA,
        ],
        compiler_params=pltpu.CompilerParams(vmem_limit_bytes=46 << 20),
        cost_estimate=pl.CostEstimate(flops=2 * size * 32 * 1024 * 512, bytes_accessed=size * 131072, transcendentals=0),
        name="half_transform",
    )(pair_blocks, integrals, occ)


def load(src, dst, sem, parts):
    step = src.shape[0] // parts
    return [
        pltpu.make_async_copy(src.at[pl.ds(k * step, step)], dst.at[pl.ds(k * step, step)], sem.at[k])
        for k in range(parts)
    ]


def tiles(metric_ref, rows, sem, start, size):
    return [
        pltpu.make_async_copy(
            metric_ref.at[:, pl.ds(start, size), pl.ds(n * TILE, TILE)], rows.at[:, :, pl.ds(n * TILE, TILE)], sem.at[n]
        )
        for n in range(NAUX // TILE)
    ]


def slabs(src, dst, sem):
    return [
        pltpu.make_async_copy(src.at[:, pl.ds(n * TILE, TILE)], dst.at[:, pl.ds(n * TILE, TILE)], sem.at[n])
        for n in range(NAUX // TILE)
    ]


def turn(buf, high, low):
    for r in range(4):
        t = jnp.concatenate([buf[a * 4 + r] for a in range(GROUPS)], axis=0)
        top = t.astype(BF16)
        high[r * 128 : (r + 1) * 128, :] = top.T
        if low is not None:
            low[r * 128 : (r + 1) * 128, :] = (t - top.astype(F32)).astype(BF16).T


def fit_kernel(start, size, own_ref, oth_ref, metric_ref, fit_ref, rows, buf, high, low, sem, hsem):
    depth = GROUPS * size
    metric = tiles(metric_ref, rows, sem, start, size)
    sides = [load(ref, buf.at[k], hsem.at[k], 4) for k, ref in enumerate((own_ref, oth_ref))]
    for c in (*sides[0], *sides[1], *metric):
        c.start()
    for k in range(2):
        for c in sides[k]:
            c.wait()
        turn(buf.at[k], high.at[k], low.at[k])
    for n in range(NAUX // TILE):
        metric[n].wait()
        m = rows[:, :, n * TILE : (n + 1) * TILE].reshape(depth, TILE)
        for k in range(2):
            fit_ref[k, :, n * TILE : (n + 1) * TILE] = jnp.dot(
                high[k], m, preferred_element_type=F32
            ) + jnp.dot(low[k], m, preferred_element_type=F32)


def first_fit(own, oth, metric, start, size):
    depth = GROUPS * size
    hbm = pl.BlockSpec(memory_space=pl.ANY)
    return pl.pallas_call(
        functools.partial(fit_kernel, start, size),
        out_shape=jax.ShapeDtypeStruct((2, 512, NAUX), F32),
        in_specs=[hbm, hbm, hbm],
        out_specs=pl.BlockSpec(memory_space=pltpu.VMEM),
        scratch_shapes=[
            pltpu.VMEM((GROUPS, size, NAUX), BF16),
            pltpu.VMEM((2, 64, size, 128), F32),
            pltpu.VMEM((2, 512, depth), BF16),
            pltpu.VMEM((2, 512, depth), BF16),
            pltpu.SemaphoreType.DMA((NAUX // TILE,)),
            pltpu.SemaphoreType.DMA((2, 4)),
        ],
        compiler_params=pltpu.CompilerParams(vmem_limit_bytes=46 << 20),
        cost_estimate=pl.CostEstimate(flops=4 * depth * NAUX * 1024, bytes_accessed=24 << 20, transcendentals=0),
        name="first_fit",
    )(own, oth, metric)


def own_kernel(start, size, h_ref, part_ref, metric_ref, fit_ref, rows, buf, part, high, sem, hsem, psem):
    depth = GROUPS * size
    metric = tiles(metric_ref, rows, sem, start, size)
    side = load(h_ref, buf, hsem, 4)
    add = slabs(part_ref.at[0], part, psem)
    for c in (*side, *(c for pair in zip(metric, add) for c in pair)):
        c.start()
    for c in side:
        c.wait()
    turn(buf, high, None)
    for n in range(NAUX // TILE):
        metric[n].wait()
        add[n].wait()
        at = slice(n * TILE, (n + 1) * TILE)
        m = rows[:, :, at].reshape(depth, TILE)
        f = part[:, at] + jnp.dot(high[...], m, preferred_element_type=F32)
        top = f.astype(BF16)
        fit_ref[0, :, at] = top
        fit_ref[1, :, at] = (f - top.astype(F32)).astype(BF16)


def own_fit(own, part, metric, start, size):
    depth = GROUPS * size
    hbm = pl.BlockSpec(memory_space=pl.ANY)
    return pl.pallas_call(
        functools.partial(own_kernel, start, size),
        out_shape=jax.ShapeDtypeStruct((2, 512, NAUX), BF16),
        in_specs=[hbm, hbm, hbm],
        out_specs=pl.BlockSpec(memory_space=pltpu.VMEM),
        scratch_shapes=[
            pltpu.VMEM((GROUPS, size, NAUX), BF16),
            pltpu.VMEM((64, size, 128), F32),
            pltpu.VMEM((512, NAUX), F32),
            pltpu.VMEM((512, depth), BF16),
            pltpu.SemaphoreType.DMA((NAUX // TILE,)),
            pltpu.SemaphoreType.DMA((4,)),
            pltpu.SemaphoreType.DMA((NAUX // TILE,)),
        ],
        compiler_params=pltpu.CompilerParams(vmem_limit_bytes=46 << 20),
        cost_estimate=pl.CostEstimate(flops=2 * depth * NAUX * 512, bytes_accessed=16 << 20, transcendentals=0),
        name="own_fit",
    )(own, part, metric)


def last_kernel(
    start, size, h_ref, part_ref, fit_ref, metric_ref, out_ref, rows, buf, part, own, high, fit, sem, hsem, psem, osem
):
    depth = GROUPS * size
    metric = tiles(metric_ref, rows, sem, start, size)
    side = load(h_ref, buf, hsem, 4)
    add = slabs(part_ref.at[1], part, psem)
    mine = pltpu.make_async_copy(fit_ref, own, osem)
    for c in (*side, *(c for pair in zip(metric, add) for c in pair), mine):
        c.start()
    for c in side:
        c.wait()
    turn(buf, high, None)
    for n in range(NAUX // TILE):
        metric[n].wait()
        add[n].wait()
        at = slice(n * TILE, (n + 1) * TILE)
        m = rows[:, :, at].reshape(depth, TILE)
        fit[:, at] = (part[:, at] + jnp.dot(high[...], m, preferred_element_type=F32)).astype(BF16)
    mine.wait()

    core = lax.axis_index("col")
    for other in range(2):
        half = lax.rem(core + other, 2)
        f = fit[...] if other else own[0]
        k = lax.dot_general(f, own[0], (((1,), (1,)), ((), ())), preferred_element_type=F32)
        k = k + lax.dot_general(f, own[1], (((1,), (1,)), ((), ())), preferred_element_type=F32)
        part[:, :512] = k
        for y in range(4):
            for b in range(2):
                for z in range(4):
                    chip = (y * 4 + half * 2 + b) * 4 + z
                    for c in range(2):
                        for m2 in range(2):
                            top = y * 128 + b * 64 + m2 * 32 + c * 16
                            out_ref[chip * 2 + c, m2 * 16 : (m2 + 1) * 16, :] = part[
                                top : top + 16, z * 128 : (z + 1) * 128
                            ]


def last_fit(oth, part, fit, metric, start, size):
    depth = GROUPS * size
    hbm = pl.BlockSpec(memory_space=pl.ANY)
    return pl.pallas_call(
        functools.partial(last_kernel, start, size),
        out_shape=jax.ShapeDtypeStruct((128, 32, 128), F32),
        in_specs=[hbm, hbm, hbm, hbm],
        out_specs=pl.BlockSpec(memory_space=pltpu.VMEM),
        scratch_shapes=[
            pltpu.VMEM((GROUPS, size, NAUX), BF16),
            pltpu.VMEM((64, size, 128), F32),
            pltpu.VMEM((512, NAUX), F32),
            pltpu.VMEM((2, 512, NAUX), BF16),
            pltpu.VMEM((512, depth), BF16),
            pltpu.VMEM((512, NAUX), BF16),
            pltpu.SemaphoreType.DMA((NAUX // TILE,)),
            pltpu.SemaphoreType.DMA((4,)),
            pltpu.SemaphoreType.DMA((NAUX // TILE,)),
            pltpu.SemaphoreType.DMA,
        ],
        compiler_params=pltpu.CompilerParams(vmem_limit_bytes=36 << 20),
        cost_estimate=pl.CostEstimate(flops=2 * depth * NAUX * 512, bytes_accessed=16 << 20, transcendentals=0),
        name="last_fit",
    )(oth, part, fit, metric)


def sum_kernel(x_ref, out_ref):
    lane_in = lax.broadcasted_iota(jnp.int32, (128, 128), 0)
    lane_out = lax.broadcasted_iota(jnp.int32, (128, 128), 1)
    src = (lane_out // 64) * 64 + lax.rem(lane_out, 2) * 32 + lax.rem(lane_out, 64) // 2
    right = jnp.where(lane_in == src, 1.0, 0.0)
    row_out = lax.broadcasted_iota(jnp.int32, (32, 32), 0)
    row_in = lax.broadcasted_iota(jnp.int32, (32, 32), 1)
    left = jnp.where(row_in == lax.rem(row_out, 2) * 16 + row_out // 2, 1.0, 0.0)
    for h in range(2):
        total = jnp.sum(x_ref[:, h], axis=0)
        total = jnp.dot(total, right, precision=lax.Precision.HIGHEST, preferred_element_type=F32)
        total = jnp.dot(left, total, precision=lax.Precision.HIGHEST, preferred_element_type=F32)
        out_ref[:, h * 128 : (h + 1) * 128] = total


def sum_chips(x):
    return pl.pallas_call(
        sum_kernel,
        out_shape=jax.ShapeDtypeStruct((32, 256), F32),
        compiler_params=pltpu.CompilerParams(vmem_limit_bytes=16 << 20),
        name="sum_chips",
    )(x.reshape(64, 2, 32, 128))


def body(integrals, pair_blocks, occupied, metric):
    occ = occupied.T
    metric = metric.reshape(GROUPS, AUX, NAUX)
    swap = [(0, 1), (1, 0)]
    halves = []
    for start, size in CHUNKS:
        mine, other = half_transform(integrals, pair_blocks, occ, start, size)
        h = mine + lax.ppermute(other, "col", swap)
        if not halves:
            h, pair_blocks = lax.optimization_barrier((h, pair_blocks))
            own = lax.all_to_all(h, ("aux", "row"), 0, 0)
        halves.append(h)
    last = lax.all_to_all(h, ("aux", "row"), 0, 0)
    part = first_fit(own, lax.ppermute(own, "col", swap), metric, *CHUNKS[0])
    last, part = lax.optimization_barrier((last, part))
    crossed = lax.ppermute(last, "col", swap)
    fit = own_fit(last, part, metric, *CHUNKS[1])
    k = last_fit(crossed, part, fit, metric, *CHUNKS[1])
    k = lax.all_to_all(k, ("aux", "row", "col"), 0, 0)
    return sum_chips(k).T


def solution(mesh):
    return jax.shard_map(
        body,
        mesh=mesh,
        in_specs=(P("aux", ("row", "col"), None), P(None, ("row", "col")), P("col", None), P()),
        out_specs=P("row", ("aux", "col")),
        check_vma=False,
    )
```

```python
import functools

import jax
import jax.numpy as jnp
from jax import lax
from jax.experimental import pallas as pl
from jax.experimental.pallas import tpu as pltpu
from jax.sharding import PartitionSpec as P

BS = 64
SLOT = 8
NOCC = 64
NAUX = 2560
AUX = 160
GROUPS = 16
CHUNKS = ((0, 80), (80, 80))
PB = 16
TILE = 512
F32 = jnp.float32
BF16 = jnp.bfloat16


def build_weights(pairs, occ_ref, weights):
    core = lax.axis_index("col")
    row = lax.broadcasted_iota(jnp.int32, (8 * BS, 2 * BS), 0)
    lane = lax.broadcasted_iota(jnp.int32, (8 * BS, 2 * BS), 1)
    own = lax.broadcasted_iota(jnp.int32, (BS, 2 * BS), 1)
    for s in range(SLOT):
        b, e = pairs[0, s], pairs[1, s]
        local_b = jnp.where(b >= 0, lax.rem(b + 64, 4), 0)
        local_e = lax.rem(e + 64, 8)
        place = lax.rem(local_b // 2 + core, 2) * 2 + lax.rem(local_b, 2)
        place = jnp.where(b >= 0, place, -1)
        pick = jnp.where(row == local_e * BS + lax.rem(lane, BS), 1.0, 0.0).astype(BF16)
        c = jnp.dot(occ_ref[...], pick, preferred_element_type=F32)
        for hb in range(4):
            keep = jnp.where(place == hb, 1.0, 0.0)
            for m2 in range(2):
                part = jnp.where(own // BS == m2, c, 0.0) * keep
                at = (hb * 2 + m2) * BS
                weights[at : at + BS, s * 128 : (s + 1) * 128] = part.astype(BF16)


def gather_slots(x_ref, wide, rhs):
    for j in range(32):
        wide[:, j] = x_ref[:, :, j * 128 : (j + 1) * 128].astype(F32)
    flat = wide.reshape(PB * 32 * SLOT, 128)
    for s in range(SLOT):
        rhs[:, s * 128 : (s + 1) * 128] = flat[pl.ds(s, PB * 32, stride=SLOT), :].astype(BF16)


def spread(prod, ref, first, size):
    lane = lax.broadcasted_iota(jnp.int32, (NOCC, 128), 1)
    low64 = lane < 64
    low32 = lax.rem(lane, 64) < 32
    out = ref.reshape(NOCC * size, 128)
    for q in range(PB // 4):
        t = [prod[v * BS : (v + 1) * BS, q * 128 : (q + 1) * 128] for v in range(4)]
        r = [pltpu.roll(jnp.where(low64, t[v + 2], t[v]), 64, 1) for v in range(2)]
        a0, a1 = (jnp.where(low64, t[v], r[v]) for v in range(2))
        a2, a3 = (jnp.where(low64, r[v], t[v + 2]) for v in range(2))
        for p, (u, v) in enumerate(((a0, a1), (a2, a3))):
            at = first + q * 4 + p * 2
            out[pl.ds(at, NOCC, stride=size), :] = jnp.where(low32, u, pltpu.roll(v, 32, 1))
            out[pl.ds(at + 1, NOCC, stride=size), :] = jnp.where(low32, pltpu.roll(u, 96, 1), v)


def times(w, x):
    return lax.dot_general(w, x, (((1,), (1,)), ((), ())), preferred_element_type=F32)


def fetch(start, size, x_ref, occ_hbm, x_buf, occ_ref, sem, osem):
    copies = [
        pltpu.make_async_copy(x_ref.at[pl.ds(start + g * PB, PB)], x_buf.at[pl.ds(g * PB, PB)], sem.at[g])
        for g in range(size // PB)
    ]
    first = pltpu.make_async_copy(occ_hbm, occ_ref, osem)
    first.start()
    for c in copies:
        c.start()
    first.wait()
    return copies


def both_kernel(start, size, pairs, x_ref, occ_hbm, mine, other, weights, x_buf, wide, rhs, prod, occ, sem, osem):
    copies = fetch(start, size, x_ref, occ_hbm, x_buf, occ, sem, osem)
    build_weights(pairs, occ, weights)
    for g in range(size // PB):
        k = g % 2
        copies[g].wait()
        gather_slots(x_buf.at[pl.ds(g * PB, PB)], wide.at[k], rhs.at[k])
        prod[k] = times(weights[...], rhs[k])
        spread(prod.at[k, pl.ds(0, 4 * BS)], mine, g * PB, size)
        spread(prod.at[k, pl.ds(4 * BS, 4 * BS)], other, g * PB, size)


def other_kernel(start, size, pairs, x_ref, occ_hbm, other, rhs, weights, x_buf, wide, prod, occ, sem, osem):
    copies = fetch(start, size, x_ref, occ_hbm, x_buf, occ, sem, osem)
    build_weights(pairs, occ, weights)
    for g in range(size // PB):
        k = g % 2
        copies[g].wait()
        gather_slots(x_buf.at[pl.ds(g * PB, PB)], wide.at[k], rhs.at[g])
        prod[k] = times(weights[4 * BS :, :], rhs[g])
        spread(prod.at[k], other, g * PB, size)


def mine_kernel(size, rhs, weights, mine, prod):
    for g in range(size // PB):
        prod[g % 2] = times(weights[: 4 * BS, :], rhs[g])
        spread(prod.at[g % 2], mine, g * PB, size)


def half_transform(integrals, pair_blocks, occ, start, size, split):
    steps = size // PB
    half = jax.ShapeDtypeStruct((NOCC, size, 128), F32)
    vm = pl.BlockSpec(memory_space=pltpu.VMEM)
    hbm = pl.BlockSpec(memory_space=pltpu.HBM)
    scratch = [
        pltpu.VMEM((size, SLOT, BS * BS), BF16),
        pltpu.VMEM((2, PB, 32, SLOT, 128), F32),
        pltpu.VMEM((2, 4 * BS if split else 8 * BS, PB * 32), F32),
        pltpu.VMEM((NOCC, 8 * BS), BF16),
        pltpu.SemaphoreType.DMA((steps,)),
        pltpu.SemaphoreType.DMA,
    ]
    cost = pl.CostEstimate(flops=2 * size * 32 * 1024 * 512, bytes_accessed=size * 131072, transcendentals=0)
    if not split:
        scratch.insert(0, pltpu.VMEM((8 * BS, SLOT * 128), BF16))
        scratch.insert(3, pltpu.VMEM((2, PB * 32, SLOT * 128), BF16))
        return pl.pallas_call(
            functools.partial(both_kernel, start, size),
            out_shape=(half, half),
            in_specs=[pl.BlockSpec(memory_space=pltpu.SMEM), hbm, hbm],
            out_specs=(vm, vm),
            scratch_shapes=scratch,
            compiler_params=pltpu.CompilerParams(vmem_limit_bytes=46 << 20),
            cost_estimate=cost,
            name="half_both",
        )(pair_blocks, integrals, occ)
    other, rhs, weights = pl.pallas_call(
        functools.partial(other_kernel, start, size),
        out_shape=(
            half,
            jax.ShapeDtypeStruct((steps, PB * 32, SLOT * 128), BF16),
            jax.ShapeDtypeStruct((8 * BS, SLOT * 128), BF16),
        ),
        in_specs=[pl.BlockSpec(memory_space=pltpu.SMEM), hbm, hbm],
        out_specs=(vm, vm, vm),
        scratch_shapes=scratch,
        compiler_params=pltpu.CompilerParams(vmem_limit_bytes=44 << 20),
        cost_estimate=cost,
        name="half_other",
    )(pair_blocks, integrals, occ)
    mine = pl.pallas_call(
        functools.partial(mine_kernel, size),
        out_shape=half,
        in_specs=[vm, vm],
        out_specs=vm,
        scratch_shapes=[pltpu.VMEM((2, 4 * BS, PB * 32), F32)],
        compiler_params=pltpu.CompilerParams(vmem_limit_bytes=24 << 20),
        cost_estimate=cost,
        name="half_mine",
    )(rhs, weights)
    return mine, other


def load(src, dst, sem, parts):
    step = src.shape[0] // parts
    return [
        pltpu.make_async_copy(src.at[pl.ds(k * step, step)], dst.at[pl.ds(k * step, step)], sem.at[k])
        for k in range(parts)
    ]


def tiles(metric_ref, rows, sem, start, size):
    return [
        pltpu.make_async_copy(
            metric_ref.at[:, pl.ds(start, size), pl.ds(n * TILE, TILE)], rows.at[:, :, pl.ds(n * TILE, TILE)], sem.at[n]
        )
        for n in range(NAUX // TILE)
    ]


def slabs(src, dst, sem):
    return [
        pltpu.make_async_copy(src.at[:, pl.ds(n * TILE, TILE)], dst.at[:, pl.ds(n * TILE, TILE)], sem.at[n])
        for n in range(NAUX // TILE)
    ]


def turn(buf, high, low):
    for r in range(4):
        t = jnp.concatenate([buf[a * 4 + r] for a in range(GROUPS)], axis=0)
        top = t.astype(BF16)
        high[r * 128 : (r + 1) * 128, :] = top.T
        if low is not None:
            low[r * 128 : (r + 1) * 128, :] = (t - top.astype(F32)).astype(BF16).T


def fit_kernel(start, size, own_ref, oth_ref, metric_ref, fit_ref, rows, buf, high, low, sem, hsem):
    depth = GROUPS * size
    metric = tiles(metric_ref, rows, sem, start, size)
    sides = [load(ref, buf.at[k], hsem.at[k], 4) for k, ref in enumerate((own_ref, oth_ref))]
    for c in (*sides[0], *sides[1], *metric):
        c.start()
    for k in range(2):
        for c in sides[k]:
            c.wait()
        turn(buf.at[k], high.at[k], low.at[k])
    for n in range(NAUX // TILE):
        metric[n].wait()
        m = rows[:, :, n * TILE : (n + 1) * TILE].reshape(depth, TILE)
        for k in range(2):
            fit_ref[k, :, n * TILE : (n + 1) * TILE] = jnp.dot(
                high[k], m, preferred_element_type=F32
            ) + jnp.dot(low[k], m, preferred_element_type=F32)


def first_fit(own, oth, metric, start, size):
    depth = GROUPS * size
    hbm = pl.BlockSpec(memory_space=pl.ANY)
    return pl.pallas_call(
        functools.partial(fit_kernel, start, size),
        out_shape=jax.ShapeDtypeStruct((2, 512, NAUX), F32),
        in_specs=[hbm, hbm, hbm],
        out_specs=pl.BlockSpec(memory_space=pltpu.VMEM),
        scratch_shapes=[
            pltpu.VMEM((GROUPS, size, NAUX), BF16),
            pltpu.VMEM((2, 64, size, 128), F32),
            pltpu.VMEM((2, 512, depth), BF16),
            pltpu.VMEM((2, 512, depth), BF16),
            pltpu.SemaphoreType.DMA((NAUX // TILE,)),
            pltpu.SemaphoreType.DMA((2, 4)),
        ],
        compiler_params=pltpu.CompilerParams(vmem_limit_bytes=46 << 20),
        cost_estimate=pl.CostEstimate(flops=4 * depth * NAUX * 1024, bytes_accessed=24 << 20, transcendentals=0),
        name="first_fit",
    )(own, oth, metric)


def own_kernel(start, size, h_ref, part_ref, metric_ref, fit_ref, rows, buf, part, high, sem, hsem, psem):
    depth = GROUPS * size
    metric = tiles(metric_ref, rows, sem, start, size)
    side = load(h_ref, buf, hsem, 4)
    add = slabs(part_ref.at[0], part, psem)
    for c in (*side, *(c for pair in zip(metric, add) for c in pair)):
        c.start()
    for c in side:
        c.wait()
    turn(buf, high, None)
    for n in range(NAUX // TILE):
        metric[n].wait()
        add[n].wait()
        at = slice(n * TILE, (n + 1) * TILE)
        m = rows[:, :, at].reshape(depth, TILE)
        f = part[:, at] + jnp.dot(high[...], m, preferred_element_type=F32)
        top = f.astype(BF16)
        fit_ref[0, :, at] = top
        fit_ref[1, :, at] = (f - top.astype(F32)).astype(BF16)


def own_fit(own, part, metric, start, size):
    depth = GROUPS * size
    hbm = pl.BlockSpec(memory_space=pl.ANY)
    return pl.pallas_call(
        functools.partial(own_kernel, start, size),
        out_shape=jax.ShapeDtypeStruct((2, 512, NAUX), BF16),
        in_specs=[hbm, hbm, hbm],
        out_specs=pl.BlockSpec(memory_space=pltpu.VMEM),
        scratch_shapes=[
            pltpu.VMEM((GROUPS, size, NAUX), BF16),
            pltpu.VMEM((64, size, 128), F32),
            pltpu.VMEM((512, NAUX), F32),
            pltpu.VMEM((512, depth), BF16),
            pltpu.SemaphoreType.DMA((NAUX // TILE,)),
            pltpu.SemaphoreType.DMA((4,)),
            pltpu.SemaphoreType.DMA((NAUX // TILE,)),
        ],
        compiler_params=pltpu.CompilerParams(vmem_limit_bytes=46 << 20),
        cost_estimate=pl.CostEstimate(flops=2 * depth * NAUX * 512, bytes_accessed=16 << 20, transcendentals=0),
        name="own_fit",
    )(own, part, metric)


def last_kernel(
    start, size, h_ref, part_ref, fit_ref, metric_ref, out_ref, rows, buf, part, high, fit, whole, own, sem, hsem, psem, osem
):
    depth = GROUPS * size
    metric = tiles(metric_ref, rows, sem, start, size)
    side = load(h_ref, buf, hsem, 4)
    add = slabs(part_ref.at[1], part, psem)
    mine = pltpu.make_async_copy(fit_ref, own, osem)
    for c in (mine, *side, *(c for pair in zip(metric, add) for c in pair)):
        c.start()

    core = lax.axis_index("col")

    def finish(other, f):
        half = lax.rem(core + other, 2)
        whole[...] = times(f, own[0]) + times(f, own[1])
        for y in range(4):
            for b in range(2):
                for z in range(4):
                    chip = (y * 4 + half * 2 + b) * 4 + z
                    for c in range(2):
                        for m2 in range(2):
                            top = y * 128 + b * 64 + m2 * 32 + c * 16
                            out_ref[chip * 2 + c, m2 * 16 : (m2 + 1) * 16, :] = whole[
                                top : top + 16, z * 128 : (z + 1) * 128
                            ]

    mine.wait()
    finish(0, own[0])
    for c in side:
        c.wait()
    turn(buf, high, None)
    for n in range(NAUX // TILE):
        metric[n].wait()
        add[n].wait()
        at = slice(n * TILE, (n + 1) * TILE)
        m = rows[:, :, at].reshape(depth, TILE)
        fit[:, at] = (part[:, at] + jnp.dot(high[...], m, preferred_element_type=F32)).astype(BF16)
    finish(1, fit[...])

def last_fit(oth, part, fit, metric, start, size):
    depth = GROUPS * size
    hbm = pl.BlockSpec(memory_space=pl.ANY)
    return pl.pallas_call(
        functools.partial(last_kernel, start, size),
        out_shape=jax.ShapeDtypeStruct((128, 32, 128), F32),
        in_specs=[hbm, hbm, hbm, hbm],
        out_specs=pl.BlockSpec(memory_space=pltpu.VMEM),
        scratch_shapes=[
            pltpu.VMEM((GROUPS, size, NAUX), BF16),
            pltpu.VMEM((64, size, 128), F32),
            pltpu.VMEM((512, NAUX), F32),
            pltpu.VMEM((512, depth), BF16),
            pltpu.VMEM((512, NAUX), BF16),
            pltpu.VMEM((512, 512), F32),
            pltpu.VMEM((2, 512, NAUX), BF16),
            pltpu.SemaphoreType.DMA((NAUX // TILE,)),
            pltpu.SemaphoreType.DMA((4,)),
            pltpu.SemaphoreType.DMA((NAUX // TILE,)),
            pltpu.SemaphoreType.DMA,
        ],
        compiler_params=pltpu.CompilerParams(vmem_limit_bytes=36 << 20),
        cost_estimate=pl.CostEstimate(flops=2 * depth * NAUX * 512, bytes_accessed=16 << 20, transcendentals=0),
        name="last_fit",
    )(oth, part, fit, metric)


def sum_kernel(x_ref, out_ref):
    lane_in = lax.broadcasted_iota(jnp.int32, (128, 128), 0)
    lane_out = lax.broadcasted_iota(jnp.int32, (128, 128), 1)
    src = (lane_out // 64) * 64 + lax.rem(lane_out, 2) * 32 + lax.rem(lane_out, 64) // 2
    right = jnp.where(lane_in == src, 1.0, 0.0)
    row_out = lax.broadcasted_iota(jnp.int32, (32, 32), 0)
    row_in = lax.broadcasted_iota(jnp.int32, (32, 32), 1)
    left = jnp.where(row_in == lax.rem(row_out, 2) * 16 + row_out // 2, 1.0, 0.0)
    for h in range(2):
        total = jnp.sum(x_ref[:, h], axis=0)
        total = jnp.dot(total, right, precision=lax.Precision.HIGHEST, preferred_element_type=F32)
        total = jnp.dot(left, total, precision=lax.Precision.HIGHEST, preferred_element_type=F32)
        out_ref[:, h * 128 : (h + 1) * 128] = total


def sum_chips(x):
    return pl.pallas_call(
        sum_kernel,
        out_shape=jax.ShapeDtypeStruct((32, 256), F32),
        compiler_params=pltpu.CompilerParams(vmem_limit_bytes=16 << 20),
        name="sum_chips",
    )(x.reshape(64, 2, 32, 128))


def body(integrals, pair_blocks, occupied, metric):
    occ = occupied.T
    metric = metric.reshape(GROUPS, AUX, NAUX)
    swap = [(0, 1), (1, 0)]
    halves = []
    for start, size in CHUNKS:
        mine, other = half_transform(integrals, pair_blocks, occ, start, size, not halves)
        h = mine + lax.ppermute(other, "col", swap)
        if not halves:
            h, pair_blocks = lax.optimization_barrier((h, pair_blocks))
            own = lax.all_to_all(h, ("aux", "row"), 0, 0)
        halves.append(h)
    last = lax.all_to_all(h, ("aux", "row"), 0, 0)
    part = first_fit(own, lax.ppermute(own, "col", swap), metric, *CHUNKS[0])
    last, part = lax.optimization_barrier((last, part))
    crossed = lax.ppermute(last, "col", swap)
    fit = own_fit(last, part, metric, *CHUNKS[1])
    k = last_fit(crossed, part, fit, metric, *CHUNKS[1])
    k = lax.all_to_all(k, ("aux", "row", "col"), 0, 0)
    return sum_chips(k).T


def solution(mesh):
    return jax.shard_map(
        body,
        mesh=mesh,
        in_specs=(P("aux", ("row", "col"), None), P(None, ("row", "col")), P("col", None), P()),
        out_specs=P("row", ("aux", "col")),
        check_vma=False,
    )
```

```python
import functools

import jax
import jax.numpy as jnp
from jax import lax
from jax.experimental import pallas as pl
from jax.experimental.pallas import tpu as pltpu
from jax.sharding import PartitionSpec as P

BS = 64
SLOT = 8
NOCC = 64
NAUX = 2560
AUX = 160
GROUPS = 16
CHUNKS = ((0, 96), (96, 64))
PB = 16
TILE = 512
F32 = jnp.float32
BF16 = jnp.bfloat16


def build_weights(pairs, occ_ref, weights):
    core = lax.axis_index("col")
    row = lax.broadcasted_iota(jnp.int32, (8 * BS, 2 * BS), 0)
    lane = lax.broadcasted_iota(jnp.int32, (8 * BS, 2 * BS), 1)
    own = lax.broadcasted_iota(jnp.int32, (BS, 2 * BS), 1)
    for s in range(SLOT):
        b, e = pairs[0, s], pairs[1, s]
        local_b = jnp.where(b >= 0, lax.rem(b + 64, 4), 0)
        local_e = lax.rem(e + 64, 8)
        place = lax.rem(local_b // 2 + core, 2) * 2 + lax.rem(local_b, 2)
        place = jnp.where(b >= 0, place, -1)
        pick = jnp.where(row == local_e * BS + lax.rem(lane, BS), 1.0, 0.0).astype(BF16)
        c = jnp.dot(occ_ref[...], pick, preferred_element_type=F32)
        for hb in range(4):
            keep = jnp.where(place == hb, 1.0, 0.0)
            for m2 in range(2):
                part = jnp.where(own // BS == m2, c, 0.0) * keep
                at = (hb * 2 + m2) * BS
                weights[at : at + BS, s * 128 : (s + 1) * 128] = part.astype(BF16)


def gather_slots(x_ref, wide, rhs):
    for j in range(32):
        wide[:, j] = x_ref[:, :, j * 128 : (j + 1) * 128].astype(F32)
    flat = wide.reshape(PB * 32 * SLOT, 128)
    for s in range(SLOT):
        rhs[:, s * 128 : (s + 1) * 128] = flat[pl.ds(s, PB * 32, stride=SLOT), :].astype(BF16)


def spread(prod, ref, first, size):
    lane = lax.broadcasted_iota(jnp.int32, (NOCC, 128), 1)
    low64 = lane < 64
    low32 = lax.rem(lane, 64) < 32
    out = ref.reshape(NOCC * size, 128)
    for q in range(PB // 4):
        t = [prod[v * BS : (v + 1) * BS, q * 128 : (q + 1) * 128] for v in range(4)]
        r = [pltpu.roll(jnp.where(low64, t[v + 2], t[v]), 64, 1) for v in range(2)]
        a0, a1 = (jnp.where(low64, t[v], r[v]) for v in range(2))
        a2, a3 = (jnp.where(low64, r[v], t[v + 2]) for v in range(2))
        for p, (u, v) in enumerate(((a0, a1), (a2, a3))):
            at = first + q * 4 + p * 2
            out[pl.ds(at, NOCC, stride=size), :] = jnp.where(low32, u, pltpu.roll(v, 32, 1))
            out[pl.ds(at + 1, NOCC, stride=size), :] = jnp.where(low32, pltpu.roll(u, 96, 1), v)


def times(w, x):
    return lax.dot_general(w, x, (((1,), (1,)), ((), ())), preferred_element_type=F32)


def fetch(start, size, x_ref, occ_hbm, x_buf, occ_ref, sem, osem):
    copies = [
        pltpu.make_async_copy(x_ref.at[pl.ds(start + g * PB, PB)], x_buf.at[pl.ds(g * PB, PB)], sem.at[g])
        for g in range(size // PB)
    ]
    first = pltpu.make_async_copy(occ_hbm, occ_ref, osem)
    first.start()
    for c in copies:
        c.start()
    first.wait()
    return copies


def both_kernel(start, size, pairs, x_ref, occ_hbm, mine, other, weights, x_buf, wide, rhs, prod, occ, sem, osem):
    copies = fetch(start, size, x_ref, occ_hbm, x_buf, occ, sem, osem)
    build_weights(pairs, occ, weights)
    for g in range(size // PB):
        k = g % 2
        copies[g].wait()
        gather_slots(x_buf.at[pl.ds(g * PB, PB)], wide.at[k], rhs.at[k])
        prod[k] = times(weights[...], rhs[k])
        spread(prod.at[k, pl.ds(0, 4 * BS)], mine, g * PB, size)
        spread(prod.at[k, pl.ds(4 * BS, 4 * BS)], other, g * PB, size)


def other_kernel(start, size, pairs, x_ref, occ_hbm, other, rhs, weights, x_buf, wide, prod, occ, sem, osem):
    copies = fetch(start, size, x_ref, occ_hbm, x_buf, occ, sem, osem)
    build_weights(pairs, occ, weights)
    for g in range(size // PB):
        k = g % 2
        copies[g].wait()
        gather_slots(x_buf.at[pl.ds(g * PB, PB)], wide.at[k], rhs.at[g])
        prod[k] = times(weights[4 * BS :, :], rhs[g])
        spread(prod.at[k], other, g * PB, size)


def mine_kernel(size, rhs, weights, mine, prod):
    for g in range(size // PB):
        prod[g % 2] = times(weights[: 4 * BS, :], rhs[g])
        spread(prod.at[g % 2], mine, g * PB, size)


def half_transform(integrals, pair_blocks, occ, start, size, split):
    steps = size // PB
    half = jax.ShapeDtypeStruct((NOCC, size, 128), F32)
    vm = pl.BlockSpec(memory_space=pltpu.VMEM)
    hbm = pl.BlockSpec(memory_space=pltpu.HBM)
    scratch = [
        pltpu.VMEM((size, SLOT, BS * BS), BF16),
        pltpu.VMEM((2, PB, 32, SLOT, 128), F32),
        pltpu.VMEM((2, 4 * BS if split else 8 * BS, PB * 32), F32),
        pltpu.VMEM((NOCC, 8 * BS), BF16),
        pltpu.SemaphoreType.DMA((steps,)),
        pltpu.SemaphoreType.DMA,
    ]
    cost = pl.CostEstimate(flops=2 * size * 32 * 1024 * 512, bytes_accessed=size * 131072, transcendentals=0)
    if not split:
        scratch.insert(0, pltpu.VMEM((8 * BS, SLOT * 128), BF16))
        scratch.insert(3, pltpu.VMEM((2, PB * 32, SLOT * 128), BF16))
        return pl.pallas_call(
            functools.partial(both_kernel, start, size),
            out_shape=(half, half),
            in_specs=[pl.BlockSpec(memory_space=pltpu.SMEM), hbm, hbm],
            out_specs=(vm, vm),
            scratch_shapes=scratch,
            compiler_params=pltpu.CompilerParams(vmem_limit_bytes=46 << 20),
            cost_estimate=cost,
            name="half_both",
        )(pair_blocks, integrals, occ)
    other, rhs, weights = pl.pallas_call(
        functools.partial(other_kernel, start, size),
        out_shape=(
            half,
            jax.ShapeDtypeStruct((steps, PB * 32, SLOT * 128), BF16),
            jax.ShapeDtypeStruct((8 * BS, SLOT * 128), BF16),
        ),
        in_specs=[pl.BlockSpec(memory_space=pltpu.SMEM), hbm, hbm],
        out_specs=(vm, vm, vm),
        scratch_shapes=scratch,
        compiler_params=pltpu.CompilerParams(vmem_limit_bytes=40 << 20),
        cost_estimate=cost,
        name="half_other",
    )(pair_blocks, integrals, occ)
    mine = pl.pallas_call(
        functools.partial(mine_kernel, size),
        out_shape=half,
        in_specs=[vm, vm],
        out_specs=vm,
        scratch_shapes=[pltpu.VMEM((2, 4 * BS, PB * 32), F32)],
        compiler_params=pltpu.CompilerParams(vmem_limit_bytes=24 << 20),
        cost_estimate=cost,
        name="half_mine",
    )(rhs, weights)
    return mine, other


def load(src, dst, sem, parts):
    step = src.shape[0] // parts
    return [
        pltpu.make_async_copy(src.at[pl.ds(k * step, step)], dst.at[pl.ds(k * step, step)], sem.at[k])
        for k in range(parts)
    ]


def tiles(metric_ref, rows, sem, start, size):
    return [
        pltpu.make_async_copy(
            metric_ref.at[:, pl.ds(start, size), pl.ds(n * TILE, TILE)], rows.at[:, :, pl.ds(n * TILE, TILE)], sem.at[n]
        )
        for n in range(NAUX // TILE)
    ]


def slabs(src, dst, sem):
    return [
        pltpu.make_async_copy(src.at[:, pl.ds(n * TILE, TILE)], dst.at[:, pl.ds(n * TILE, TILE)], sem.at[n])
        for n in range(NAUX // TILE)
    ]


def turn(buf, high, low):
    for r in range(4):
        t = jnp.concatenate([buf[a * 4 + r] for a in range(GROUPS)], axis=0)
        top = t.astype(BF16)
        high[r * 128 : (r + 1) * 128, :] = top.T
        if low is not None:
            low[r * 128 : (r + 1) * 128, :] = (t - top.astype(F32)).astype(BF16).T


def fit_kernel(start, size, own_ref, oth_ref, metric_ref, fit_ref, rows, buf, high, low, sem, hsem):
    depth = GROUPS * size
    metric = tiles(metric_ref, rows, sem, start, size)
    sides = [load(ref, buf.at[k], hsem.at[k], 4) for k, ref in enumerate((own_ref, oth_ref))]
    for c in (*sides[0], *sides[1], *metric):
        c.start()
    for k in range(2):
        for c in sides[k]:
            c.wait()
        turn(buf.at[k], high.at[k], low.at[k])
    for n in range(NAUX // TILE):
        metric[n].wait()
        m = rows[:, :, n * TILE : (n + 1) * TILE].reshape(depth, TILE)
        for k in range(2):
            fit_ref[k, :, n * TILE : (n + 1) * TILE] = jnp.dot(
                high[k], m, preferred_element_type=F32
            ) + jnp.dot(low[k], m, preferred_element_type=F32)


def first_fit(own, oth, metric, start, size):
    depth = GROUPS * size
    hbm = pl.BlockSpec(memory_space=pl.ANY)
    return pl.pallas_call(
        functools.partial(fit_kernel, start, size),
        out_shape=jax.ShapeDtypeStruct((2, 512, NAUX), F32),
        in_specs=[hbm, hbm, hbm],
        out_specs=pl.BlockSpec(memory_space=pltpu.VMEM),
        scratch_shapes=[
            pltpu.VMEM((GROUPS, size, NAUX), BF16),
            pltpu.VMEM((2, 64, size, 128), F32),
            pltpu.VMEM((2, 512, depth), BF16),
            pltpu.VMEM((2, 512, depth), BF16),
            pltpu.SemaphoreType.DMA((NAUX // TILE,)),
            pltpu.SemaphoreType.DMA((2, 4)),
        ],
        compiler_params=pltpu.CompilerParams(vmem_limit_bytes=46 << 20),
        cost_estimate=pl.CostEstimate(flops=4 * depth * NAUX * 1024, bytes_accessed=24 << 20, transcendentals=0),
        name="first_fit",
    )(own, oth, metric)


def own_kernel(start, size, h_ref, part_ref, metric_ref, fit_ref, rows, buf, part, high, sem, hsem, psem):
    depth = GROUPS * size
    metric = tiles(metric_ref, rows, sem, start, size)
    side = load(h_ref, buf, hsem, 4)
    add = slabs(part_ref.at[0], part, psem)
    for c in (*side, *(c for pair in zip(metric, add) for c in pair)):
        c.start()
    for c in side:
        c.wait()
    turn(buf, high, None)
    for n in range(NAUX // TILE):
        metric[n].wait()
        add[n].wait()
        at = slice(n * TILE, (n + 1) * TILE)
        m = rows[:, :, at].reshape(depth, TILE)
        f = part[:, at] + jnp.dot(high[...], m, preferred_element_type=F32)
        top = f.astype(BF16)
        fit_ref[0, :, at] = top
        fit_ref[1, :, at] = (f - top.astype(F32)).astype(BF16)


def own_fit(own, part, metric, start, size):
    depth = GROUPS * size
    hbm = pl.BlockSpec(memory_space=pl.ANY)
    return pl.pallas_call(
        functools.partial(own_kernel, start, size),
        out_shape=jax.ShapeDtypeStruct((2, 512, NAUX), BF16),
        in_specs=[hbm, hbm, hbm],
        out_specs=pl.BlockSpec(memory_space=pltpu.VMEM),
        scratch_shapes=[
            pltpu.VMEM((GROUPS, size, NAUX), BF16),
            pltpu.VMEM((64, size, 128), F32),
            pltpu.VMEM((512, NAUX), F32),
            pltpu.VMEM((512, depth), BF16),
            pltpu.SemaphoreType.DMA((NAUX // TILE,)),
            pltpu.SemaphoreType.DMA((4,)),
            pltpu.SemaphoreType.DMA((NAUX // TILE,)),
        ],
        compiler_params=pltpu.CompilerParams(vmem_limit_bytes=46 << 20),
        cost_estimate=pl.CostEstimate(flops=2 * depth * NAUX * 512, bytes_accessed=16 << 20, transcendentals=0),
        name="own_fit",
    )(own, part, metric)


def last_kernel(
    start, size, h_ref, part_ref, fit_ref, metric_ref, out_ref, rows, buf, part, high, fit, whole, own, sem, hsem, psem, osem
):
    depth = GROUPS * size
    metric = tiles(metric_ref, rows, sem, start, size)
    side = load(h_ref, buf, hsem, 4)
    add = slabs(part_ref.at[1], part, psem)
    mine = pltpu.make_async_copy(fit_ref, own, osem)
    for c in (mine, *side, *(c for pair in zip(metric, add) for c in pair)):
        c.start()

    core = lax.axis_index("col")

    def finish(other, f):
        half = lax.rem(core + other, 2)
        whole[...] = times(f, own[0]) + times(f, own[1])
        for y in range(4):
            for b in range(2):
                for z in range(4):
                    chip = (y * 4 + half * 2 + b) * 4 + z
                    for c in range(2):
                        for m2 in range(2):
                            top = y * 128 + b * 64 + m2 * 32 + c * 16
                            out_ref[chip * 2 + c, m2 * 16 : (m2 + 1) * 16, :] = whole[
                                top : top + 16, z * 128 : (z + 1) * 128
                            ]

    mine.wait()
    finish(0, own[0])
    for c in side:
        c.wait()
    turn(buf, high, None)
    for n in range(NAUX // TILE):
        metric[n].wait()
        add[n].wait()
        at = slice(n * TILE, (n + 1) * TILE)
        m = rows[:, :, at].reshape(depth, TILE)
        fit[:, at] = (part[:, at] + jnp.dot(high[...], m, preferred_element_type=F32)).astype(BF16)
    finish(1, fit[...])

def last_fit(oth, part, fit, metric, start, size):
    depth = GROUPS * size
    hbm = pl.BlockSpec(memory_space=pl.ANY)
    return pl.pallas_call(
        functools.partial(last_kernel, start, size),
        out_shape=jax.ShapeDtypeStruct((128, 32, 128), F32),
        in_specs=[hbm, hbm, hbm, hbm],
        out_specs=pl.BlockSpec(memory_space=pltpu.VMEM),
        scratch_shapes=[
            pltpu.VMEM((GROUPS, size, NAUX), BF16),
            pltpu.VMEM((64, size, 128), F32),
            pltpu.VMEM((512, NAUX), F32),
            pltpu.VMEM((512, depth), BF16),
            pltpu.VMEM((512, NAUX), BF16),
            pltpu.VMEM((512, 512), F32),
            pltpu.VMEM((2, 512, NAUX), BF16),
            pltpu.SemaphoreType.DMA((NAUX // TILE,)),
            pltpu.SemaphoreType.DMA((4,)),
            pltpu.SemaphoreType.DMA((NAUX // TILE,)),
            pltpu.SemaphoreType.DMA,
        ],
        compiler_params=pltpu.CompilerParams(vmem_limit_bytes=36 << 20),
        cost_estimate=pl.CostEstimate(flops=2 * depth * NAUX * 512, bytes_accessed=16 << 20, transcendentals=0),
        name="last_fit",
    )(oth, part, fit, metric)


def sum_kernel(x_ref, out_ref):
    lane_in = lax.broadcasted_iota(jnp.int32, (128, 128), 0)
    lane_out = lax.broadcasted_iota(jnp.int32, (128, 128), 1)
    src = (lane_out // 64) * 64 + lax.rem(lane_out, 2) * 32 + lax.rem(lane_out, 64) // 2
    right = jnp.where(lane_in == src, 1.0, 0.0)
    row_out = lax.broadcasted_iota(jnp.int32, (32, 32), 0)
    row_in = lax.broadcasted_iota(jnp.int32, (32, 32), 1)
    left = jnp.where(row_in == lax.rem(row_out, 2) * 16 + row_out // 2, 1.0, 0.0)
    for h in range(2):
        total = jnp.sum(x_ref[:, h], axis=0)
        total = jnp.dot(total, right, precision=lax.Precision.HIGHEST, preferred_element_type=F32)
        total = jnp.dot(left, total, precision=lax.Precision.HIGHEST, preferred_element_type=F32)
        out_ref[:, h * 128 : (h + 1) * 128] = total


def sum_chips(x):
    return pl.pallas_call(
        sum_kernel,
        out_shape=jax.ShapeDtypeStruct((32, 256), F32),
        compiler_params=pltpu.CompilerParams(vmem_limit_bytes=16 << 20),
        name="sum_chips",
    )(x.reshape(64, 2, 32, 128))


def body(integrals, pair_blocks, occupied, metric):
    occ = occupied.T
    metric = metric.reshape(GROUPS, AUX, NAUX)
    swap = [(0, 1), (1, 0)]
    halves = []
    for start, size in CHUNKS:
        mine, other = half_transform(integrals, pair_blocks, occ, start, size, not halves)
        h = mine + lax.ppermute(other, "col", swap)
        if not halves:
            h, pair_blocks = lax.optimization_barrier((h, pair_blocks))
            own = lax.all_to_all(h, ("aux", "row"), 0, 0)
        halves.append(h)
    last = lax.all_to_all(h, ("aux", "row"), 0, 0)
    part = first_fit(own, lax.ppermute(own, "col", swap), metric, *CHUNKS[0])
    last, part = lax.optimization_barrier((last, part))
    crossed = lax.ppermute(last, "col", swap)
    fit = own_fit(last, part, metric, *CHUNKS[1])
    k = last_fit(crossed, part, fit, metric, *CHUNKS[1])
    k = lax.all_to_all(k, ("aux", "row", "col"), 0, 0)
    return sum_chips(k).T


def solution(mesh):
    return jax.shard_map(
        body,
        mesh=mesh,
        in_specs=(P("aux", ("row", "col"), None), P(None, ("row", "col")), P("col", None), P()),
        out_specs=P("row", ("aux", "col")),
        check_vma=False,
    )
```
